32 devices in a mesh: group: 2 (over y), ctx: 4 (over z), head: 2 (over x), sub: 2 (over core).
Axes of the slice: x: 2, y: 2, z: 4, core: 2. Of those that a mesh axis runs over, the one named last changes fastest.
Arguments:
- q_lin: bfloat16 [2048, 32, 128], P(('group', 'ctx'), ('head', 'sub')), parts along dimension 0, may hold values from -1.796875 to 1.796875
- k_lin: bfloat16 [2048, 32, 128], P(('group', 'ctx'), ('head', 'sub')), parts along dimension 0, may hold values from -1.796875 to 1.796875
- v_lin: bfloat16 [2048, 32, 128], P(('group', 'ctx'), ('head', 'sub')), parts along dimension 0, may hold values from -6 to 6
- decay_log: float32 [2048, 32], P(('group', 'ctx'), ('head', 'sub')), parts along dimension 0, may hold values from -0.7 to 0, as said below
- q_soft: bfloat16 [2048, 32, 128], P(('group', 'ctx'), ('head', 'sub')), parts along dimension 0, may hold values from -8 to 8, as said below
- k_soft: bfloat16 [2048, 8, 128], P(('group', 'ctx'), ('head', 'sub')), parts along dimension 0, may hold values from -8 to 8, as said below
- v_soft: bfloat16 [2048, 8, 128], P(('group', 'ctx'), ('head', 'sub')), parts along dimension 0, may hold values from -6 to 6
- doc_starts: int32 [12], P('group'), parts along dimension 0, may hold values from 0 to 768, as said below
Outputs:
- lin_out: bfloat16 [2048, 32, 128], P(('group', 'ctx'), ('head', 'sub')), parts along dimension 0
- soft_out: bfloat16 [2048, 32, 128], P(('group', 'ctx'), ('head', 'sub')), parts along dimension 0
The draws below stay inside these ranges and needn't reach their ends.
There are 2 independent parts, one for each index of `group`. The reference program is written for one: setup_inputs(seed, part) draws one part's arguments, and reference() takes and returns one part's arrays. A program takes and returns all parts, laid end to end along the dimension named above; each array names one. Nothing has to cross between parts.
Inputs may be any that keep to these rules, and one draw needn't show every extreme that they name: `decay_log`: entries are negative. `q_soft`: entries are at most 8 in magnitude. `k_soft`: entries are at most 8 in magnitude. `doc_starts`: starts never fall and are multiples of 256; equal starts (empty documents) may occur. The first is 0, the last is 768, and all others lie at or after position (3) * 256.
All inputs are finite; a program needn't handle non-finite values.
Results may differ from the reference program's by a relative error of at most 0.0075.
Values may be sent and summed in bfloat16 or wider, within the bound.
A program may use at most 64 MiB of HBM per device.

```python
import math
import jax
import jax.numpy as jnp
from jax import lax

SLICE_LENGTH = 256
GRAIN = 256
HDIM = 128
QHEADS = 32
KVHEADS = 8
LHEADS = 32
BUNDLE_LENGTH = 1024
NDOCS = 6
N_CTX = 4


def query_key_pair(key):
    base = jax.random.fold_in(key, 101)
    key_a, key_b = jax.random.split(base, 2)
    keys = jnp.clip(1.58 * jax.random.normal(key_a, (BUNDLE_LENGTH, KVHEADS, HDIM), jnp.float32), -8.0, 8.0)
    queries = jnp.clip(1.58 * jax.random.normal(key_b, (BUNDLE_LENGTH, QHEADS, HDIM), jnp.float32), -8.0, 8.0)
    return (queries, keys)


def draw_q_soft(key, part):
    queries, keys = query_key_pair(key)
    return queries.astype(jnp.bfloat16)


def draw_k_soft(key, part):
    queries, keys = query_key_pair(key)
    return keys.astype(jnp.bfloat16)


def draw_decay_log(key, part):
    base = jax.random.fold_in(key, 202)
    key_a, key_b, key_c, key_d, key_e, seed_handle_six, key_g = jax.random.split(base, 7)
    share = 0.5
    quick = jax.random.uniform(key_a, (LHEADS,)) < share
    quick_rate = jnp.exp(jax.random.uniform(key_b, (LHEADS,), jnp.float32, math.log(1.0 / 50.0), math.log(1.0 / 30.0)))
    slow_rate = jnp.exp(jax.random.uniform(key_c, (LHEADS,), jnp.float32, math.log(0.3 / BUNDLE_LENGTH), math.log(0.6 / BUNDLE_LENGTH)))
    forgetting_speed = jnp.where(quick, quick_rate, slow_rate)
    blocks = BUNDLE_LENGTH // SLICE_LENGTH
    segment_scaling = jax.random.uniform(key_d, (blocks, LHEADS), jnp.float32, 0.6, 1.4)
    position_scaling = jax.random.uniform(key_e, (BUNDLE_LENGTH, LHEADS), jnp.float32, 0.7, 1.4)
    slice_locations = jnp.arange(BUNDLE_LENGTH)
    position_groups = jax.random.randint(seed_handle_six, (2,), 0, BUNDLE_LENGTH)
    recursion_level_count = jax.random.uniform(key_g, (2,), jnp.float32, 0.22, 0.6)
    position_group = jnp.sum(jnp.where(slice_locations[:, None] == position_groups[None, :], recursion_level_count[None, :], 0.0), axis=1)
    content_vectors = -(forgetting_speed[None, :] * segment_scaling[slice_locations // SLICE_LENGTH] * position_scaling) - position_group[:, None]
    return content_vectors.astype(jnp.float32)


def draw_doc_starts(key, part):
    base = jax.random.fold_in(key, 303)
    grains = BUNDLE_LENGTH // GRAIN
    lowest = (N_CTX // 2 + 1) * (SLICE_LENGTH // GRAIN)
    picked = jnp.sort(jax.random.randint(base, (NDOCS - 2,), lowest, grains).astype(jnp.int32))
    starts = jnp.concatenate([jnp.zeros((1,), jnp.int32), picked, jnp.full((1,), grains - 1, jnp.int32)])
    return (starts * GRAIN).astype(jnp.int32)


def steps_of(rng, extent, shards, low, top_value):
    def one(position, blocks):
        steps = jax.random.uniform(jax.random.fold_in(jax.random.fold_in(rng, 6), position), (blocks,), jnp.float32, low / len(shards), top_value / len(shards))
        return jnp.repeat(jnp.exp(steps), extent[position] // blocks).reshape((-1,) + (1,) * (len(extent) - position - 1))

    gain = one(*shards[0])
    for cut in shards[1:]:
        gain = gain * one(*cut)
    return gain


def noise(stream_key, dims, spread, bound, cuts=(), kind=jnp.bfloat16):
    loudness = steps_of(stream_key, dims, cuts, -0.22, 0.18) if cuts else 1.0
    values = jax.random.normal(stream_key, dims, jnp.float32) * spread * loudness
    return jnp.minimum(jnp.maximum(values, -bound), bound).astype(kind)


def setup_inputs(seed: int = 0, part: int = 0) -> dict:
    splits = jax.random.split(jax.random.key(seed), 9)
    part_splits = jax.random.split(jax.random.fold_in(splits[8], part), 9)
    return {
        "q_lin": noise(part_splits[0], (BUNDLE_LENGTH, LHEADS, HDIM), 0.3, 1.796875, ((0, 4), (1, 4))),
        "k_lin": noise(part_splits[1], (BUNDLE_LENGTH, LHEADS, HDIM), 0.3, 1.796875, ((0, 4), (1, 4))),
        "v_lin": noise(part_splits[2], (BUNDLE_LENGTH, LHEADS, HDIM), 1.0, 6.0, ((0, 4), (1, 4))),
        "decay_log": draw_decay_log(jax.random.fold_in(jax.random.fold_in(splits[8], part), 71), part),
        "q_soft": draw_q_soft(jax.random.fold_in(jax.random.fold_in(splits[8], part), 71), part),
        "k_soft": draw_k_soft(jax.random.fold_in(jax.random.fold_in(splits[8], part), 71), part),
        "v_soft": noise(part_splits[6], (BUNDLE_LENGTH, KVHEADS, HDIM), 1.0, 6.0, ((0, 4), (1, 4))),
        "doc_starts": draw_doc_starts(jax.random.fold_in(jax.random.fold_in(splits[8], part), 71), part),
    }


def doc_index(slice_locations, doc_starts):
    return lax.optimization_barrier(jnp.sum((doc_starts[None, :] <= slice_locations[:, None]).astype(jnp.int32), axis=1)) - 1

def lightning_block(q_part, k_part, v_part, a_part, state):
    rise = jnp.cumsum(a_part, axis=0)
    q_full = q_part.astype(jnp.float32)
    k_full = k_part.astype(jnp.float32)
    v_full = v_part.astype(jnp.float32)
    scores = jnp.einsum('ihd,jhd->hij', q_full, k_full)
    rows = jnp.arange(q_part.shape[0])
    lower = (rows[:, None] >= rows[None, :])[None]
    gap = rise.T[:, :, None] - rise.T[:, None, :]
    fade = jnp.where(lower, jnp.exp(jnp.where(lower, gap, 0.0)), 0.0)
    inner = lax.optimization_barrier((scores * fade).astype(jnp.bfloat16)).astype(jnp.float32)
    intra = jnp.einsum('hij,jhd->ihd', inner, v_full)
    lead = q_full * jnp.exp(rise)[:, :, None]
    inter = jnp.einsum('ihd,hde->ihe', lead, state, precision=lax.Precision.HIGHEST)
    total = intra + inter
    normed = total * lax.rsqrt(lax.optimization_barrier(jnp.mean(total * total, axis=-1, keepdims=True)) + 1e-06)
    block_decay = rise[-1]
    tail = k_full * jnp.exp(block_decay[None, :] - rise)[:, :, None]
    tail = lax.optimization_barrier(tail.astype(jnp.bfloat16)).astype(jnp.float32)
    local_state = jnp.einsum('jhd,jhe->hde', tail, v_full)
    return (normed.astype(jnp.bfloat16), block_decay, local_state)

def lightning_layer(q_lin, k_lin, v_lin, decay_log, doc_starts):
    blocks = BUNDLE_LENGTH // SLICE_LENGTH
    q_b = q_lin.reshape(blocks, SLICE_LENGTH, LHEADS, HDIM)
    k_b = k_lin.reshape(blocks, SLICE_LENGTH, LHEADS, HDIM)
    v_b = v_lin.reshape(blocks, SLICE_LENGTH, LHEADS, HDIM)
    a_b = decay_log.reshape(blocks, SLICE_LENGTH, LHEADS)
    firsts = jnp.arange(blocks, dtype=jnp.int32) * SLICE_LENGTH
    keep = doc_index(firsts, doc_starts) == doc_index(firsts + SLICE_LENGTH, doc_starts)

    def advance(state, inputs):
        q_part, k_part, v_part, a_part, keep_one = inputs
        normed, block_decay, local_state = lightning_block(q_part, k_part, v_part, a_part, state)
        state_next = jnp.exp(block_decay)[:, None, None] * state + local_state
        state_next = jnp.where(keep_one, state_next, jnp.zeros_like(state_next))
        return (state_next, normed)
    start = jnp.zeros((LHEADS, HDIM, HDIM), jnp.float32)
    last, outputs = lax.scan(advance, start, (q_b, k_b, v_b, a_b, keep))
    return outputs.reshape(BUNDLE_LENGTH, LHEADS, HDIM)

def softmax_layer(q_soft, k_soft, v_soft, doc_starts):
    group = QHEADS // KVHEADS
    scale = 1.0 / math.sqrt(HDIM)
    keys = k_soft.astype(jnp.float32)
    content_vectors = v_soft.astype(jnp.float32)
    slice_locations = jnp.arange(BUNDLE_LENGTH, dtype=jnp.int32)
    key_doc = doc_index(slice_locations, doc_starts)

    def one(block):
        q_part = lax.dynamic_slice_in_dim(q_soft, block * SLICE_LENGTH, SLICE_LENGTH, 0)
        q_part = q_part.astype(jnp.float32).reshape(SLICE_LENGTH, KVHEADS, group, HDIM)
        q_pos = block * SLICE_LENGTH + jnp.arange(SLICE_LENGTH, dtype=jnp.int32)
        q_doc = doc_index(q_pos, doc_starts)
        allowed = (slice_locations[None, :] <= q_pos[:, None]) & (key_doc[None, :] == q_doc[:, None])
        scores = jnp.einsum('tkgd,skd->tkgs', q_part, keys) * scale
        scores = jnp.where(allowed[:, None, None, :], scores, -jnp.inf)
        top = lax.optimization_barrier(jnp.max(scores, axis=-1, keepdims=True))
        weights = jnp.exp(scores - top)
        total = lax.optimization_barrier(jnp.sum(weights, axis=-1))
        rounded = lax.optimization_barrier(weights.astype(jnp.bfloat16)).astype(jnp.float32)
        mixed = jnp.einsum('tkgs,skd->tkgd', rounded, content_vectors) / total[..., None]
        return mixed.reshape(SLICE_LENGTH, QHEADS, HDIM).astype(jnp.bfloat16)
    outputs = lax.map(one, jnp.arange(BUNDLE_LENGTH // SLICE_LENGTH, dtype=jnp.int32))
    return outputs.reshape(BUNDLE_LENGTH, QHEADS, HDIM)

def reference(q_lin, k_lin, v_lin, decay_log, q_soft, k_soft, v_soft, doc_starts):
    lin_out = lightning_layer(q_lin, k_lin, v_lin, decay_log, doc_starts)
    soft_out = softmax_layer(q_soft, k_soft, v_soft, doc_starts)
    return (lin_out, soft_out)
```

```python
import functools
import math

import jax
import jax.numpy as jnp
from jax import lax
from jax.experimental import pallas as pl
from jax.experimental.pallas import tpu as pltpu
from jax.sharding import PartitionSpec as P

MESH = pl.DeviceIdType.MESH
F32, BF16 = jnp.float32, jnp.bfloat16
NEVER = -1e30


def dot(a, b, contract):
    return lax.dot_general(a, b, ((contract[:1], contract[1:]), ((), ())), preferred_element_type=F32)


def kernel(n, tok, heads, kv_heads, share, chunk, starts, ql_hbm, kl_hbm, vl_hbm, decay_hbm, qs_hbm, ks_hbm, vs_hbm,
           lin_hbm, soft_hbm,
           ql, kl, vl, decay, qs, ks, vs, lin_out, soft_out,
           k_held, v_held, s_held, s_own, local_state, wide, q_head, k_head, v_head, intra, top, acc,
           in_sems, out_sems, own_sems, pass_sems, kv_sems, s_send, s_recv):
    me = lax.axis_index("ctx")
    sends = me < n - 2
    takes = (me > 0) & (me < n - 1)
    right, left = me + 1, me - 1
    rows, cols = tok * heads, tok * kv_heads

    barrier = pltpu.get_barrier_semaphore()

    @pl.when(sends)
    def _():
        pl.semaphore_signal(barrier, inc=1, device_id={"ctx": right}, device_id_type=MESH)

    @pl.when(takes)
    def _():
        pl.semaphore_signal(barrier, inc=1, device_id={"ctx": left}, device_id_type=MESH)

    loads = [
        pltpu.make_async_copy(src, dst, in_sems.at[i])
        for i, (src, dst) in enumerate(
            [(decay_hbm, decay), (kl_hbm, kl), (vl_hbm, vl), (ql_hbm, ql), (qs_hbm, qs), (ks_hbm, ks), (vs_hbm, vs)]
        )
    ]
    for load in loads:
        load.start()

    @pl.when(sends & takes)
    def _():
        pl.semaphore_wait(barrier, 2)

    @pl.when(sends != takes)
    def _():
        pl.semaphore_wait(barrier, 1)

    def push(src, dst, send_sem, recv_sem):
        return pltpu.make_async_remote_copy(
            src_ref=src, dst_ref=dst, send_sem=send_sem, recv_sem=recv_sem,
            device_id={"ctx": right}, device_id_type=MESH,
        )

    def own_pushes():
        return (
            push(ks_hbm, k_held.at[me], own_sems.at[0], kv_sems.at[me, 0]),
            push(vs_hbm, v_held.at[me], own_sems.at[1], kv_sems.at[me, 1]),
        )

    def passes(slot):
        return (
            push(k_held.at[slot], k_held.at[slot], pass_sems.at[slot, 0], kv_sems.at[slot, 0]),
            push(v_held.at[slot], v_held.at[slot], pass_sems.at[slot, 1], kv_sems.at[slot, 1]),
        )

    def state_push(c):
        part = pl.ds(c * chunk, chunk)
        return push(s_own.at[part], s_held.at[part], s_send.at[c], s_recv.at[c])

    @pl.when(sends)
    def _():
        for copy in own_pushes():
            copy.start()

    def doc_of(position):
        return sum((starts[i] <= position).astype(jnp.int32) for i in range(starts.shape[0]))

    my_doc = doc_of(me * tok)
    keep_next = jnp.where(my_doc == doc_of((me + 1) * tok), 1.0, 0.0).astype(F32)

    loads[0].wait()
    d = decay[...]
    d1 = d.astype(BF16)
    rest = d - d1.astype(F32)
    d2 = rest.astype(BF16)
    d3 = (rest - d2.astype(F32)).astype(BF16)
    i_row = lax.broadcasted_iota(jnp.int32, (tok, tok), 0)
    i_col = lax.broadcasted_iota(jnp.int32, (tok, tok), 1)
    lower = i_row >= i_col
    tri = jnp.where(lower, 1.0, 0.0).astype(BF16)
    rise = dot(tri, d1, (1, 1)) + dot(tri, d2, (1, 1)) + dot(tri, d3, (1, 1))
    rise_t = dot(d1, tri, (1, 1)) + dot(d2, tri, (1, 1)) + dot(d3, tri, (1, 1))
    last = rise[tok - 1 :, :]
    to_end = jnp.exp(last - rise)
    from_start = jnp.exp(rise)
    block_factor = jnp.exp(last)

    def by_head(src, dst):
        wide[...] = src[...].astype(F32)
        for h in range(heads):
            dst[h] = wide[pl.ds(h, tok, stride=heads), :].astype(BF16)

    loads[1].wait()
    by_head(kl, k_head)
    loads[2].wait()
    by_head(vl, v_head)

    @pl.when(sends)
    def _():
        for h in range(heads):
            tail = (k_head[h].astype(F32) * to_end[:, h : h + 1]).astype(BF16)
            local_state[h] = dot(tail, v_head[h], (0, 0))

    @pl.when(me == 0)
    def _():
        for c in range(heads // chunk):
            for h in range(c * chunk, (c + 1) * chunk):
                s_own[h] = (keep_next * local_state[h]).astype(BF16)
            state_push(c).start()

    c2 = math.log2(math.e) / math.sqrt(qs.shape[1])
    tile = min(256, rows)
    part_rows = lax.broadcasted_iota(jnp.int32, (tile, cols), 0)
    part_cols = lax.broadcasted_iota(jnp.int32, (tile, cols), 1)
    ones = jnp.ones((cols, qs.shape[1]), BF16)

    def own_block():
        def step(i, _):
            at = pl.ds(pl.multiple_of(i * tile, tile), tile)
            s = dot(qs[at, :], ks[...], (1, 1))
            fits = (part_rows % heads) // share == part_cols % kv_heads
            past = part_cols // kv_heads <= i * (tile // heads) + part_rows // heads
            s = jnp.where(fits & past, s, NEVER)
            high = jnp.max(s, axis=1, keepdims=True)
            p = jnp.exp2((s - high) * c2).astype(BF16)
            top[at, :] = jnp.broadcast_to(high, (tile, 128))
            acc[at, :] = dot(p, jnp.concatenate([vs[...], ones], axis=1), (1, 0))
            return 0

        lax.fori_loop(0, rows // tile, step, 0)

    def held_block(slot):
        bias = jnp.where(doc_of(slot * tok) == my_doc, 0.0, NEVER).astype(F32)

        def step(i, _):
            at = pl.ds(pl.multiple_of(i * tile, tile), tile)
            s = dot(qs[at, :], k_held[slot], (1, 1))
            fits = (part_rows % heads) // share == part_cols % kv_heads
            s = jnp.where(fits, s + bias, NEVER)
            before = top[at, :]
            high = jnp.maximum(before, jnp.max(s, axis=1, keepdims=True))
            p = jnp.exp2((s - high[:, :1]) * c2).astype(BF16)
            shrink = jnp.exp2((before - high) * c2)
            top[at, :] = high
            acc[at, :] = acc[at, :] * jnp.concatenate([shrink, shrink], axis=1) + dot(
                p, jnp.concatenate([v_held[slot], ones], axis=1), (1, 0)
            )
            return 0

        lax.fori_loop(0, rows // tile, step, 0)

    def arrive(slot):
        for incoming, outgoing in zip(passes(slot), passes(slot)):
            incoming.wait_recv()

            @pl.when(sends)
            def _():
                outgoing.start()

    for load in loads[4:]:
        load.wait()
    own_block()

    @pl.when(takes)
    def _():
        arrive(me - 1)

    loads[3].wait()
    by_head(ql, q_head)
    for h in range(heads):
        gap = jnp.where(lower, rise[:, h : h + 1] - rise_t[h : h + 1, :], NEVER)
        inner = (dot(q_head[h], k_head[h], (1, 1)) * jnp.exp(gap)).astype(BF16)
        intra[h] = dot(inner, v_head[h], (1, 0))

    @pl.when(takes)
    def _():
        held_block(me - 1)

        def step(k, _):
            slot = me - k
            arrive(slot)
            held_block(slot)
            return 0

        lax.fori_loop(2, me + 1, step, 0)

    width = qs.shape[1]
    soft_out[...] = (acc[:, :width] / acc[:, width:]).astype(BF16)
    soft_store = pltpu.make_async_copy(soft_out, soft_hbm, out_sems.at[0])
    soft_store.start()

    def finish(h, total):
        size = jnp.mean(total * total, axis=1, keepdims=True)
        wide[pl.ds(h, tok, stride=heads), :] = total * lax.rsqrt(size + 1e-6)

    @pl.when(takes)
    def _():
        for c in range(heads // chunk):
            state_push(c).wait_recv()

            @pl.when(sends)
            def _():
                for h in range(c * chunk, (c + 1) * chunk):
                    joined = s_held[h].astype(F32) * block_factor[:, h : h + 1] + local_state[h]
                    s_own[h] = (keep_next * joined).astype(BF16)
                state_push(c).start()

            for h in range(c * chunk, (c + 1) * chunk):
                finish(h, intra[h] + from_start[:, h : h + 1] * dot(q_head[h], s_held[h], (1, 0)))

    @pl.when(jnp.logical_not(takes))
    def _():
        for h in range(heads):
            finish(h, intra[h])

    lin_out[...] = wide[...].astype(BF16)
    lin_store = pltpu.make_async_copy(lin_out, lin_hbm, out_sems.at[1])
    lin_store.start()

    @pl.when(sends)
    def _():
        for copy in own_pushes():
            copy.wait_send()
        for c in range(heads // chunk):
            state_push(c).wait_send()

        def step(slot, _):
            for copy in passes(slot):
                copy.wait_send()
            return 0

        lax.fori_loop(0, me, step, 0)

    soft_store.wait()
    lin_store.wait()


def on_device(n, q_lin, k_lin, v_lin, decay_log, q_soft, k_soft, v_soft, doc_starts):
    tok, heads, width = q_lin.shape
    kv_heads = k_soft.shape[1]
    rows, cols, slots = tok * heads, tok * kv_heads, max(n - 2, 1)
    chunk = 2
    flat = lambda x: x.reshape(-1, width)
    hbm = pl.BlockSpec(memory_space=pl.ANY)
    vmem = pltpu.VMEM
    dma = pltpu.SemaphoreType.DMA
    lin, soft = pl.pallas_call(
        functools.partial(kernel, n, tok, heads, kv_heads, q_soft.shape[1] // kv_heads, chunk),
        out_shape=[jax.ShapeDtypeStruct((rows, width), BF16)] * 2,
        in_specs=[pl.BlockSpec(memory_space=pltpu.SMEM)] + [hbm] * 7,
        out_specs=[hbm, hbm],
        scratch_shapes=[
            vmem((rows, width), BF16), vmem((rows, width), BF16), vmem((rows, width), BF16),
            vmem((heads, tok), F32), vmem((rows, width), BF16), vmem((cols, width), BF16), vmem((cols, width), BF16),
            vmem((rows, width), BF16), vmem((rows, width), BF16),
            vmem((slots, cols, width), BF16), vmem((slots, cols, width), BF16),
            vmem((heads, width, width), BF16), vmem((heads, width, width), BF16), vmem((heads, width, width), F32),
            vmem((rows, width), F32),
            vmem((heads, tok, width), BF16), vmem((heads, tok, width), BF16), vmem((heads, tok, width), BF16),
            vmem((heads, tok, width), F32),
            vmem((rows, 128), F32), vmem((rows, 2 * width), F32),
            dma((7,)), dma((2,)), dma((2,)), dma((slots, 2)), dma((slots, 2)),
            dma((heads // chunk,)), dma((heads // chunk,)),
        ],
        compiler_params=pltpu.CompilerParams(
            collective_id=0, has_side_effects=True, vmem_limit_bytes=60 * 1024 * 1024
        ),
        cost_estimate=pl.CostEstimate(flops=2_000_000_000, bytes_accessed=4_000_000, transcendentals=4_000_000),
    )(doc_starts, flat(q_lin), flat(k_lin), flat(v_lin), decay_log.T, flat(q_soft), flat(k_soft), flat(v_soft))
    return lin.reshape(q_lin.shape), soft.reshape(q_soft.shape)


def solution(mesh):
    long = P(("group", "ctx"), ("head", "sub"), None)
    return jax.shard_map(
        functools.partial(on_device, mesh.shape["ctx"]),
        mesh=mesh,
        in_specs=(long, long, long, P(("group", "ctx"), ("head", "sub")), long, long, long, P("group")),
        out_specs=(long, long),
        check_vma=False,
    )
```

```python
import functools
import math

import jax
import jax.numpy as jnp
from jax import lax
from jax.experimental import pallas as pl
from jax.experimental.pallas import tpu as pltpu
from jax.sharding import PartitionSpec as P

MESH = pl.DeviceIdType.MESH
F32, BF16 = jnp.float32, jnp.bfloat16
NEVER = -1e30


def dot(a, b, contract):
    return lax.dot_general(a, b, ((contract[:1], contract[1:]), ((), ())), preferred_element_type=F32)


def kernel(n, tok, heads, kv_heads, share, chunk, starts, ql_hbm, kl_hbm, vl_hbm, decay_hbm, qs_hbm, ks_hbm, vs_hbm,
           lin_out, soft_out,
           ql, kl, vl, decay, qs, ks, vs, q_wide, k_near, v_near,
           k_held, v_held, s_held, s_own, local_state, wide, q_head, k_head, v_head, intra, top, acc,
           in_sems, own_sems, pass_sems, kv_sems, s_send, s_recv):
    me = lax.axis_index("ctx")
    sends = me < n - 2
    takes = (me > 0) & (me < n - 1)
    right, left = me + 1, me - 1
    rows, cols = tok * heads, tok * kv_heads

    barrier = pltpu.get_barrier_semaphore()

    @pl.when(sends)
    def _():
        pl.semaphore_signal(barrier, inc=1, device_id={"ctx": right}, device_id_type=MESH)

    @pl.when(takes)
    def _():
        pl.semaphore_signal(barrier, inc=1, device_id={"ctx": left}, device_id_type=MESH)

    loads = [
        pltpu.make_async_copy(src, dst, in_sems.at[i])
        for i, (src, dst) in enumerate(
            [(decay_hbm, decay), (kl_hbm, kl), (vl_hbm, vl), (ql_hbm, ql), (qs_hbm, qs), (ks_hbm, ks), (vs_hbm, vs)]
        )
    ]
    for load in loads:
        load.start()

    @pl.when(sends & takes)
    def _():
        pl.semaphore_wait(barrier, 2)

    @pl.when(sends != takes)
    def _():
        pl.semaphore_wait(barrier, 1)

    def push(src, dst, send_sem, recv_sem):
        return pltpu.make_async_remote_copy(
            src_ref=src, dst_ref=dst, send_sem=send_sem, recv_sem=recv_sem,
            device_id={"ctx": right}, device_id_type=MESH,
        )

    def own_pushes():
        return (
            push(ks_hbm, k_held.at[me], own_sems.at[0], kv_sems.at[me, 0]),
            push(vs_hbm, v_held.at[me], own_sems.at[1], kv_sems.at[me, 1]),
        )

    def passes(slot):
        return (
            push(k_held.at[slot], k_held.at[slot], pass_sems.at[slot, 0], kv_sems.at[slot, 0]),
            push(v_held.at[slot], v_held.at[slot], pass_sems.at[slot, 1], kv_sems.at[slot, 1]),
        )

    def state_push(c):
        part = pl.ds(c * chunk, chunk)
        return push(s_own.at[part], s_held.at[part], s_send.at[c], s_recv.at[c])

    @pl.when(sends)
    def _():
        for copy in own_pushes():
            copy.start()

    def doc_of(position):
        return sum((starts[i] <= position).astype(jnp.int32) for i in range(starts.shape[0]))

    my_doc = doc_of(me * tok)
    keep_next = jnp.where(my_doc == doc_of((me + 1) * tok), 1.0, 0.0).astype(F32)

    loads[0].wait()
    d = decay[...]
    d1 = d.astype(BF16)
    rest = d - d1.astype(F32)
    d2 = rest.astype(BF16)
    d3 = (rest - d2.astype(F32)).astype(BF16)
    i_row = lax.broadcasted_iota(jnp.int32, (tok, tok), 0)
    i_col = lax.broadcasted_iota(jnp.int32, (tok, tok), 1)
    lower = i_row >= i_col
    tri = jnp.where(lower, 1.0, 0.0).astype(BF16)
    rise = dot(tri, d1, (1, 1)) + dot(tri, d2, (1, 1)) + dot(tri, d3, (1, 1))
    rise_t = dot(d1, tri, (1, 1)) + dot(d2, tri, (1, 1)) + dot(d3, tri, (1, 1))
    last = rise[tok - 1 :, :]
    to_end = jnp.exp(last - rise)
    from_start = jnp.exp(rise)
    block_factor = jnp.exp(last)

    def by_head(src, dst):
        wide[...] = src[...].astype(F32)
        for h in range(heads):
            dst[h] = wide[pl.ds(h, tok, stride=heads), :].astype(BF16)

    loads[1].wait()
    by_head(kl, k_head)
    loads[2].wait()
    by_head(vl, v_head)

    @pl.when(sends)
    def _():
        for h in range(heads):
            tail = (k_head[h].astype(F32) * to_end[:, h : h + 1]).astype(BF16)
            local_state[h] = dot(tail, v_head[h], (0, 0))

    @pl.when(me == 0)
    def _():
        for c in range(heads // chunk):
            for h in range(c * chunk, (c + 1) * chunk):
                s_own[h] = (keep_next * local_state[h]).astype(BF16)
            state_push(c).start()

    width = qs.shape[1]
    c2 = math.log2(math.e) / math.sqrt(width)
    tile = min(256, rows)
    span = tile // heads
    head_bits, share_bits = heads.bit_length() - 1, share.bit_length() - 1
    kv_of_row = (lax.broadcasted_iota(jnp.int32, (tile, width), 0) & (heads - 1)) >> share_bits
    mine = [jnp.where(kv_of_row == g, 1.0, 0.0).astype(F32) for g in range(kv_heads)]

    def spread(k_ref, v_ref):
        for src, dst in ((k_ref, k_near), (v_ref, v_near)):
            wide[pl.ds(0, cols), :] = src[...].astype(F32)
            for g in range(kv_heads):
                dst[:, g * width : (g + 1) * width] = wide[pl.ds(g, tok, stride=kv_heads), :].astype(BF16)

    def weigh(p, depth):
        both = dot(p, v_near[pl.ds(0, depth), :], (1, 0))
        own = sum(both[:, g * width : (g + 1) * width] * mine[g] for g in range(kv_heads))
        return own, both[:, kv_heads * width :]

    def own_block():
        mask_bf = [m.astype(BF16) for m in mine]
        for i in range(rows // tile):
            for g in range(kv_heads):
                q_wide[pl.ds(i * tile, tile), g * width : (g + 1) * width] = qs[pl.ds(i * tile, tile), :] * mask_bf[g]
        v_near[:, kv_heads * width :] = jnp.ones((tok, width), BF16)
        spread(ks, vs)
        for i in range(rows // tile):
            at = pl.ds(i * tile, tile)
            depth = min(tok, -(-(i + 1) * span // width) * width)
            s = dot(q_wide[at, :], k_near[pl.ds(0, depth), :], (1, 1))
            token = (lax.broadcasted_iota(jnp.int32, (tile, depth), 0) >> head_bits) + i * span
            s = jnp.where(lax.broadcasted_iota(jnp.int32, (tile, depth), 1) <= token, s, NEVER)
            high = jnp.max(s, axis=1, keepdims=True)
            p = jnp.exp2((s - high) * c2).astype(BF16)
            top[at, :] = jnp.broadcast_to(high, (tile, width))
            own, size = weigh(p, depth)
            acc[at, :width] = own
            acc[at, width:] = size

    def held_block(slot):
        bias = jnp.where(doc_of(slot * tok) == my_doc, 0.0, NEVER).astype(F32)
        spread(k_held.at[slot], v_held.at[slot])

        for i in range(rows // tile):
            at = pl.ds(i * tile, tile)
            s = dot(q_wide[at, :], k_near[...], (1, 1)) + bias
            before = top[at, :]
            high = jnp.maximum(before, jnp.max(s, axis=1, keepdims=True))
            p = jnp.exp2((s - high[:, :1]) * c2).astype(BF16)
            shrink = jnp.exp2((before - high) * c2)
            top[at, :] = high
            own, size = weigh(p, tok)
            acc[at, :width] = acc[at, :width] * shrink + own
            acc[at, width:] = acc[at, width:] * shrink + size

    def arrive(slot):
        for incoming, outgoing in zip(passes(slot), passes(slot)):
            incoming.wait_recv()

            @pl.when(sends)
            def _():
                outgoing.start()

    for load in loads[4:]:
        load.wait()
    own_block()

    @pl.when(takes)
    def _():
        arrive(me - 1)

    loads[3].wait()
    by_head(ql, q_head)
    for c in range(heads // chunk):
        for h in range(c * chunk, (c + 1) * chunk):
            gap = jnp.where(lower, rise[:, h : h + 1] - rise_t[h : h + 1, :], NEVER)
            inner = (dot(q_head[h], k_head[h], (1, 1)) * jnp.exp(gap)).astype(BF16)
            intra[h] = dot(inner, v_head[h], (1, 0))

        @pl.when(takes & sends)
        def _():
            state_push(c).wait_recv()
            for h in range(c * chunk, (c + 1) * chunk):
                joined = s_held[h].astype(F32) * block_factor[:, h : h + 1] + local_state[h]
                s_own[h] = (keep_next * joined).astype(BF16)
            state_push(c).start()

    @pl.when(takes)
    def _():
        held_block(me - 1)

        def step(k, _):
            slot = me - k
            arrive(slot)
            held_block(slot)
            return 0

        lax.fori_loop(2, me + 1, step, 0)

    soft_out[...] = (acc[:, :width] / acc[:, width:]).astype(BF16)

    def finish(h, total):
        size = jnp.mean(total * total, axis=1, keepdims=True)
        wide[pl.ds(h, tok, stride=heads), :] = total * lax.rsqrt(size + 1e-6)

    @pl.when(takes)
    def _():
        for c in range(heads // chunk):
            @pl.when(jnp.logical_not(sends))
            def _():
                state_push(c).wait_recv()

            for h in range(c * chunk, (c + 1) * chunk):
                finish(h, intra[h] + from_start[:, h : h + 1] * dot(q_head[h], s_held[h], (1, 0)))

    @pl.when(jnp.logical_not(takes))
    def _():
        for h in range(heads):
            finish(h, intra[h])

    lin_out[...] = wide[...].astype(BF16)

    @pl.when(sends)
    def _():
        for copy in own_pushes():
            copy.wait_send()
        for c in range(heads // chunk):
            state_push(c).wait_send()

        def step(slot, _):
            for copy in passes(slot):
                copy.wait_send()
            return 0

        lax.fori_loop(0, me, step, 0)


def on_device(n, q_lin, k_lin, v_lin, decay_log, q_soft, k_soft, v_soft, doc_starts):
    tok, heads, width = q_lin.shape
    kv_heads = k_soft.shape[1]
    rows, cols, slots = tok * heads, tok * kv_heads, max(n - 2, 1)
    chunk = 2
    flat = lambda x: x.reshape(-1, width)
    hbm = pl.BlockSpec(memory_space=pltpu.HBM)
    near = pl.BlockSpec(memory_space=pltpu.VMEM)
    vmem = pltpu.VMEM
    dma = pltpu.SemaphoreType.DMA
    lin, soft = pl.pallas_call(
        functools.partial(kernel, n, tok, heads, kv_heads, q_soft.shape[1] // kv_heads, chunk),
        out_shape=[jax.ShapeDtypeStruct((rows, width), BF16)] * 2,
        in_specs=[pl.BlockSpec(memory_space=pltpu.SMEM)] + [hbm] * 7,
        out_specs=[near, near],
        scratch_shapes=[
            vmem((rows, width), BF16), vmem((rows, width), BF16), vmem((rows, width), BF16),
            vmem((heads, tok), F32), vmem((rows, width), BF16), vmem((cols, width), BF16), vmem((cols, width), BF16),
            vmem((rows, kv_heads * width), BF16), vmem((tok, kv_heads * width), BF16), vmem((tok, (kv_heads + 1) * width), BF16),
            vmem((slots, cols, width), BF16), vmem((slots, cols, width), BF16),
            vmem((heads, width, width), BF16), vmem((heads, width, width), BF16), vmem((heads, width, width), F32),
            vmem((rows, width), F32),
            vmem((heads, tok, width), BF16), vmem((heads, tok, width), BF16), vmem((heads, tok, width), BF16),
            vmem((heads, tok, width), F32),
            vmem((rows, width), F32), vmem((rows, 2 * width), F32),
            dma((7,)), dma((2,)), dma((slots, 2)), dma((slots, 2)),
            dma((heads // chunk,)), dma((heads // chunk,)),
        ],
        compiler_params=pltpu.CompilerParams(
            collective_id=0, has_side_effects=True, vmem_limit_bytes=32 * 1024 * 1024
        ),
        cost_estimate=pl.CostEstimate(flops=2_000_000_000, bytes_accessed=4_000_000, transcendentals=4_000_000),
    )(doc_starts, flat(q_lin), flat(k_lin), flat(v_lin), decay_log.T, flat(q_soft), flat(k_soft), flat(v_soft))
    return lin.reshape(q_lin.shape), soft.reshape(q_soft.shape)


def solution(mesh):
    long = P(("group", "ctx"), ("head", "sub"), None)
    return jax.shard_map(
        functools.partial(on_device, mesh.shape["ctx"]),
        mesh=mesh,
        in_specs=(long, long, long, P(("group", "ctx"), ("head", "sub")), long, long, long, P("group")),
        out_specs=(long, long),
        check_vma=False,
    )
```

```python
import functools
import math

import jax
import jax.numpy as jnp
from jax import lax
from jax.experimental import pallas as pl
from jax.experimental.pallas import tpu as pltpu
from jax.sharding import PartitionSpec as P

MESH = pl.DeviceIdType.MESH
F32, BF16 = jnp.float32, jnp.bfloat16
NEVER = -1e30
PIECES = 4
GRANT = 60 * 1024 * 1024


def dot(a, b, contract):
    return lax.dot_general(a, b, ((contract[:1], contract[1:]), ((), ())), preferred_element_type=F32)


def kernel(n, tok, heads, kv_heads, share, chunk, starts, ql_hbm, kl_hbm, vl_hbm, decay_hbm, qs_hbm, ks_hbm, vs_hbm,
           lin_hbm, soft_hbm,
           ql, kl, vl, decay, qs, ks, vs, q_wide, k_near, v_near, lin_out, soft_out,
           k_held, v_held, s_held, s_own, local_state, wide, q_head, k_head, v_head, intra, top, acc,
           in_sems, out_sems, own_sems, pass_sems, kv_sems, s_send, s_recv):
    me = lax.axis_index("ctx")
    sends = me < n - 2
    takes = (me > 0) & (me < n - 1)
    right, left = me + 1, me - 1
    rows, cols = tok * heads, tok * kv_heads

    barrier = pltpu.get_barrier_semaphore()

    @pl.when(sends)
    def _():
        pl.semaphore_signal(barrier, inc=1, device_id={"ctx": right}, device_id_type=MESH)

    @pl.when(takes)
    def _():
        pl.semaphore_signal(barrier, inc=1, device_id={"ctx": left}, device_id_type=MESH)

    loads = [
        pltpu.make_async_copy(src, dst, in_sems.at[i])
        for i, (src, dst) in enumerate(
            [(decay_hbm, decay), (kl_hbm, kl), (vl_hbm, vl), (ql_hbm, ql), (qs_hbm, qs), (ks_hbm, ks), (vs_hbm, vs)]
        )
    ]
    for load in loads:
        load.start()

    @pl.when(sends & takes)
    def _():
        pl.semaphore_wait(barrier, 2)

    @pl.when(sends != takes)
    def _():
        pl.semaphore_wait(barrier, 1)

    def push(src, dst, send_sem, recv_sem):
        return pltpu.make_async_remote_copy(
            src_ref=src, dst_ref=dst, send_sem=send_sem, recv_sem=recv_sem,
            device_id={"ctx": right}, device_id_type=MESH,
        )

    def own_pushes():
        return (
            push(ks_hbm, k_held.at[me], own_sems.at[0], kv_sems.at[me, 0]),
            push(vs_hbm, v_held.at[me], own_sems.at[1], kv_sems.at[me, 1]),
        )

    def passes(slot):
        return (
            push(k_held.at[slot], k_held.at[slot], pass_sems.at[slot, 0], kv_sems.at[slot, 0]),
            push(v_held.at[slot], v_held.at[slot], pass_sems.at[slot, 1], kv_sems.at[slot, 1]),
        )

    def state_push(c):
        part = pl.ds(c * chunk, chunk)
        return push(s_own.at[part], s_held.at[part], s_send.at[c], s_recv.at[c])

    @pl.when(sends)
    def _():
        for copy in own_pushes():
            copy.start()

    def doc_of(position):
        return sum((starts[i] <= position).astype(jnp.int32) for i in range(starts.shape[0]))

    my_doc = doc_of(me * tok)
    keep_next = jnp.where(my_doc == doc_of((me + 1) * tok), 1.0, 0.0).astype(F32)

    loads[0].wait()
    d = decay[...]
    d1 = d.astype(BF16)
    rest = d - d1.astype(F32)
    d2 = rest.astype(BF16)
    d3 = (rest - d2.astype(F32)).astype(BF16)
    i_row = lax.broadcasted_iota(jnp.int32, (tok, tok), 0)
    i_col = lax.broadcasted_iota(jnp.int32, (tok, tok), 1)
    lower = i_row >= i_col
    tri = jnp.where(lower, 1.0, 0.0).astype(BF16)
    rise = dot(tri, d1, (1, 1)) + dot(tri, d2, (1, 1)) + dot(tri, d3, (1, 1))
    rise_t = dot(d1, tri, (1, 1)) + dot(d2, tri, (1, 1)) + dot(d3, tri, (1, 1))
    last = rise[tok - 1 :, :]
    to_end = jnp.exp(last - rise)
    from_start = jnp.exp(rise)
    block_factor = jnp.exp(last)

    def by_head(src, dst):
        wide[...] = src[...].astype(F32)
        for h in range(heads):
            dst[h] = wide[pl.ds(h, tok, stride=heads), :].astype(BF16)

    loads[1].wait()
    by_head(kl, k_head)
    loads[2].wait()
    by_head(vl, v_head)

    @pl.when(sends)
    def _():
        for h in range(heads):
            tail = (k_head[h].astype(F32) * to_end[:, h : h + 1]).astype(BF16)
            local_state[h] = dot(tail, v_head[h], (0, 0))

    @pl.when(me == 0)
    def _():
        for c in range(heads // chunk):
            for h in range(c * chunk, (c + 1) * chunk):
                s_own[h] = (keep_next * local_state[h]).astype(BF16)
            state_push(c).start()

    width = qs.shape[1]
    c2 = math.log2(math.e) / math.sqrt(width)
    tile = min(256, rows)
    span = tile // heads
    head_bits, share_bits = heads.bit_length() - 1, share.bit_length() - 1
    kv_of_row = (lax.broadcasted_iota(jnp.int32, (tile, width), 0) & (heads - 1)) >> share_bits
    mine = [jnp.where(kv_of_row == g, 1.0, 0.0).astype(F32) for g in range(kv_heads)]

    def spread(k_ref, v_ref):
        for src, dst in ((k_ref, k_near), (v_ref, v_near)):
            wide[pl.ds(0, cols), :] = src[...].astype(F32)
            for g in range(kv_heads):
                dst[:, g * width : (g + 1) * width] = wide[pl.ds(g, tok, stride=kv_heads), :].astype(BF16)

    def weigh(p, depth):
        both = dot(p, v_near[pl.ds(0, depth), :], (1, 0))
        own = sum(both[:, g * width : (g + 1) * width] * mine[g] for g in range(kv_heads))
        return own, both[:, kv_heads * width :]

    def own_block():
        mask_bf = [m.astype(BF16) for m in mine]
        for i in range(rows // tile):
            for g in range(kv_heads):
                q_wide[pl.ds(i * tile, tile), g * width : (g + 1) * width] = qs[pl.ds(i * tile, tile), :] * mask_bf[g]
        v_near[:, kv_heads * width :] = jnp.ones((tok, width), BF16)
        spread(ks, vs)
        for i in range(rows // tile):
            at = pl.ds(i * tile, tile)
            depth = min(tok, -(-(i + 1) * span // width) * width)
            s = dot(q_wide[at, :], k_near[pl.ds(0, depth), :], (1, 1))
            token = (lax.broadcasted_iota(jnp.int32, (tile, depth), 0) >> head_bits) + i * span
            s = jnp.where(lax.broadcasted_iota(jnp.int32, (tile, depth), 1) <= token, s, NEVER)
            high = jnp.max(s, axis=1, keepdims=True)
            p = jnp.exp2((s - high) * c2).astype(BF16)
            top[at, :] = jnp.broadcast_to(high, (tile, width))
            own, size = weigh(p, depth)
            acc[at, :width] = own
            acc[at, width:] = size

    def held_block(slot):
        bias = jnp.where(doc_of(slot * tok) == my_doc, 0.0, NEVER).astype(F32)
        spread(k_held.at[slot], v_held.at[slot])

        for i in range(rows // tile):
            at = pl.ds(i * tile, tile)
            s = dot(q_wide[at, :], k_near[...], (1, 1)) + bias
            before = top[at, :]
            high = jnp.maximum(before, jnp.max(s, axis=1, keepdims=True))
            p = jnp.exp2((s - high[:, :1]) * c2).astype(BF16)
            shrink = jnp.exp2((before - high) * c2)
            top[at, :] = high
            own, size = weigh(p, tok)
            acc[at, :width] = acc[at, :width] * shrink + own
            acc[at, width:] = acc[at, width:] * shrink + size

    def arrive(slot):
        for incoming, outgoing in zip(passes(slot), passes(slot)):
            incoming.wait_recv()

            @pl.when(sends)
            def _():
                outgoing.start()

    for load in loads[4:]:
        load.wait()
    own_block()

    @pl.when(takes)
    def _():
        arrive(me - 1)

    loads[3].wait()
    by_head(ql, q_head)
    for c in range(heads // chunk):
        for h in range(c * chunk, (c + 1) * chunk):
            gap = jnp.where(lower, rise[:, h : h + 1] - rise_t[h : h + 1, :], NEVER)
            inner = (dot(q_head[h], k_head[h], (1, 1)) * jnp.exp(gap)).astype(BF16)
            intra[h] = dot(inner, v_head[h], (1, 0))

        @pl.when(takes & sends)
        def _():
            state_push(c).wait_recv()
            for h in range(c * chunk, (c + 1) * chunk):
                joined = s_held[h].astype(F32) * block_factor[:, h : h + 1] + local_state[h]
                s_own[h] = (keep_next * joined).astype(BF16)
            state_push(c).start()

    @pl.when(takes)
    def _():
        held_block(me - 1)

        def step(k, _):
            slot = me - k
            arrive(slot)
            held_block(slot)
            return 0

        lax.fori_loop(2, me + 1, step, 0)

    soft_out[...] = (acc[:, :width] / acc[:, width:]).astype(BF16)
    soft_store = pltpu.make_async_copy(soft_out, soft_hbm, out_sems.at[0])
    soft_store.start()

    def finish(h, total):
        size = jnp.mean(total * total, axis=1, keepdims=True)
        wide[pl.ds(h, tok, stride=heads), :] = total * lax.rsqrt(size + 1e-6)

    @pl.when(takes)
    def _():
        for c in range(heads // chunk):
            @pl.when(jnp.logical_not(sends))
            def _():
                state_push(c).wait_recv()

            for h in range(c * chunk, (c + 1) * chunk):
                finish(h, intra[h] + from_start[:, h : h + 1] * dot(q_head[h], s_held[h], (1, 0)))

    @pl.when(jnp.logical_not(takes))
    def _():
        for h in range(heads):
            finish(h, intra[h])

    lin_out[...] = wide[...].astype(BF16)
    lin_store = pltpu.make_async_copy(lin_out, lin_hbm, out_sems.at[1])
    lin_store.start()

    @pl.when(sends)
    def _():
        for copy in own_pushes():
            copy.wait_send()
        for c in range(heads // chunk):
            state_push(c).wait_send()

        def step(slot, _):
            for copy in passes(slot):
                copy.wait_send()
            return 0

        lax.fori_loop(0, me, step, 0)

    soft_store.wait()
    lin_store.wait()


def hand_over(lin, soft, lin_out, soft_out, sems):
    size = lin.shape[0] // PIECES
    copies = [
        pltpu.make_async_copy(src.at[pl.ds(i * size, size)], dst.at[pl.ds(i * size, size)], sems.at[j, i])
        for j, (src, dst) in enumerate([(lin, lin_out), (soft, soft_out)])
        for i in range(PIECES)
    ]
    for copy in copies:
        copy.start()
    for copy in copies:
        copy.wait()


def on_device(n, q_lin, k_lin, v_lin, decay_log, q_soft, k_soft, v_soft, doc_starts):
    tok, heads, width = q_lin.shape
    kv_heads = k_soft.shape[1]
    rows, cols, slots = tok * heads, tok * kv_heads, max(n - 2, 1)
    chunk = 2
    flat = lambda x: x.reshape(-1, width)
    hbm = pl.BlockSpec(memory_space=pl.ANY)
    vmem = pltpu.VMEM
    dma = pltpu.SemaphoreType.DMA
    lin, soft = pl.pallas_call(
        functools.partial(kernel, n, tok, heads, kv_heads, q_soft.shape[1] // kv_heads, chunk),
        out_shape=[jax.ShapeDtypeStruct((rows, width), BF16)] * 2,
        in_specs=[pl.BlockSpec(memory_space=pltpu.SMEM)] + [hbm] * 7,
        out_specs=[hbm, hbm],
        scratch_shapes=[
            vmem((rows, width), BF16), vmem((rows, width), BF16), vmem((rows, width), BF16),
            vmem((heads, tok), F32), vmem((rows, width), BF16), vmem((cols, width), BF16), vmem((cols, width), BF16),
            vmem((rows, kv_heads * width), BF16), vmem((tok, kv_heads * width), BF16), vmem((tok, (kv_heads + 1) * width), BF16),
            vmem((rows, width), BF16), vmem((rows, width), BF16),
            vmem((slots, cols, width), BF16), vmem((slots, cols, width), BF16),
            vmem((heads, width, width), BF16), vmem((heads, width, width), BF16), vmem((heads, width, width), F32),
            vmem((rows, width), F32),
            vmem((heads, tok, width), BF16), vmem((heads, tok, width), BF16), vmem((heads, tok, width), BF16),
            vmem((heads, tok, width), F32),
            vmem((rows, width), F32), vmem((rows, 2 * width), F32),
            dma((7,)), dma((2,)), dma((2,)), dma((slots, 2)), dma((slots, 2)),
            dma((heads // chunk,)), dma((heads // chunk,)),
        ],
        compiler_params=pltpu.CompilerParams(
            collective_id=0, has_side_effects=True, vmem_limit_bytes=GRANT
        ),
        cost_estimate=pl.CostEstimate(flops=2_000_000_000, bytes_accessed=4_000_000, transcendentals=4_000_000),
    )(doc_starts, flat(q_lin), flat(k_lin), flat(v_lin), decay_log.T, flat(q_soft), flat(k_soft), flat(v_soft))
    lin, soft = pl.pallas_call(
        hand_over,
        out_shape=[jax.ShapeDtypeStruct((rows, width), BF16)] * 2,
        in_specs=[pl.BlockSpec(memory_space=pl.ANY)] * 2,
        out_specs=[pl.BlockSpec(memory_space=pl.ANY)] * 2,
        scratch_shapes=[dma((2, PIECES))],
        compiler_params=pltpu.CompilerParams(vmem_limit_bytes=GRANT),
    )(lin, soft)
    return lin.reshape(q_lin.shape), soft.reshape(q_soft.shape)


def solution(mesh):
    long = P(("group", "ctx"), ("head", "sub"), None)
    return jax.shard_map(
        functools.partial(on_device, mesh.shape["ctx"]),
        mesh=mesh,
        in_specs=(long, long, long, P(("group", "ctx"), ("head", "sub")), long, long, long, P("group")),
        out_specs=(long, long),
        check_vma=False,
    )
```

```python
import functools
import math

import jax
import jax.numpy as jnp
from jax import lax
from jax.experimental import pallas as pl
from jax.experimental.pallas import tpu as pltpu
from jax.sharding import PartitionSpec as P

MESH = pl.DeviceIdType.MESH
F32, BF16 = jnp.float32, jnp.bfloat16
NEVER = -1e30
PIECES = 4
GRANT = 60 * 1024 * 1024


def dot(a, b, contract):
    return lax.dot_general(a, b, ((contract[:1], contract[1:]), ((), ())), preferred_element_type=F32)


def kernel(n, tok, heads, kv_heads, share, chunk, starts, ql_hbm, kl_hbm, vl_hbm, decay_hbm, qs_hbm, ks_hbm, vs_hbm,
           lin_hbm, soft_hbm,
           ql, kl, vl, decay, qs, ks, vs, q_wide, k_near, v_near, lin_out, soft_out,
           k_held, v_held, s_held, s_own, local_state, wide, q_head, k_head, v_head, intra, top, acc,
           in_sems, out_sems, own_sems, pass_sems, kv_sems, s_send, s_recv):
    me = lax.axis_index("ctx")
    sends = me < n - 2
    takes = (me > 0) & (me < n - 1)
    right, left = me + 1, me - 1
    rows, cols = tok * heads, tok * kv_heads

    barrier = pltpu.get_barrier_semaphore()

    @pl.when(sends)
    def _():
        pl.semaphore_signal(barrier, inc=1, device_id={"ctx": right}, device_id_type=MESH)

    @pl.when(takes)
    def _():
        pl.semaphore_signal(barrier, inc=1, device_id={"ctx": left}, device_id_type=MESH)

    loads = [
        pltpu.make_async_copy(src, dst, in_sems.at[i])
        for i, (src, dst) in enumerate(
            [(decay_hbm, decay), (kl_hbm, kl), (vl_hbm, vl), (ql_hbm, ql), (qs_hbm, qs), (ks_hbm, ks), (vs_hbm, vs)]
        )
    ]
    for load in loads:
        load.start()

    @pl.when(sends & takes)
    def _():
        pl.semaphore_wait(barrier, 2)

    @pl.when(sends != takes)
    def _():
        pl.semaphore_wait(barrier, 1)

    def push(src, dst, send_sem, recv_sem):
        return pltpu.make_async_remote_copy(
            src_ref=src, dst_ref=dst, send_sem=send_sem, recv_sem=recv_sem,
            device_id={"ctx": right}, device_id_type=MESH,
        )

    def own_pushes():
        return (
            push(ks_hbm, k_held.at[me], own_sems.at[0], kv_sems.at[me, 0]),
            push(vs_hbm, v_held.at[me], own_sems.at[1], kv_sems.at[me, 1]),
        )

    def passes(slot):
        return (
            push(k_held.at[slot], k_held.at[slot], pass_sems.at[slot, 0], kv_sems.at[slot, 0]),
            push(v_held.at[slot], v_held.at[slot], pass_sems.at[slot, 1], kv_sems.at[slot, 1]),
        )

    def state_push(c):
        part = pl.ds(c * chunk, chunk)
        return push(s_own.at[part], s_held.at[part], s_send.at[c], s_recv.at[c])

    @pl.when(sends)
    def _():
        for copy in own_pushes():
            copy.start()

    def doc_of(position):
        return sum((starts[i] <= position).astype(jnp.int32) for i in range(starts.shape[0]))

    my_doc = doc_of(me * tok)
    keep_next = jnp.where(my_doc == doc_of((me + 1) * tok), 1.0, 0.0).astype(F32)

    loads[0].wait()
    d = decay[...]
    d1 = d.astype(BF16)
    rest = d - d1.astype(F32)
    d2 = rest.astype(BF16)
    d3 = (rest - d2.astype(F32)).astype(BF16)
    i_row = lax.broadcasted_iota(jnp.int32, (tok, tok), 0)
    i_col = lax.broadcasted_iota(jnp.int32, (tok, tok), 1)
    lower = i_row >= i_col
    tri = jnp.where(lower, 1.0, 0.0).astype(BF16)
    rise = dot(tri, d1, (1, 1)) + dot(tri, d2, (1, 1)) + dot(tri, d3, (1, 1))
    rise_t = dot(d1, tri, (1, 1)) + dot(d2, tri, (1, 1)) + dot(d3, tri, (1, 1))
    last = rise[tok - 1 :, :]
    to_end = jnp.exp(last - rise)
    from_start = jnp.exp(rise)
    block_factor = jnp.exp(last)

    def by_head(src, dst):
        wide[...] = src[...].astype(F32)
        for h in range(heads):
            dst[h] = wide[pl.ds(h, tok, stride=heads), :].astype(BF16)

    loads[1].wait()
    by_head(kl, k_head)
    loads[2].wait()
    by_head(vl, v_head)

    @pl.when(sends)
    def _():
        for h in range(heads):
            tail = (k_head[h].astype(F32) * to_end[:, h : h + 1]).astype(BF16)
            local_state[h] = dot(tail, v_head[h], (0, 0))

    @pl.when(me == 0)
    def _():
        for c in range(heads // chunk):
            for h in range(c * chunk, (c + 1) * chunk):
                s_own[h] = (keep_next * local_state[h]).astype(BF16)
            state_push(c).start()

    width = qs.shape[1]
    c2 = math.log2(math.e) / math.sqrt(width)
    tile = min(256, rows)
    span = tile // heads
    head_bits, share_bits = heads.bit_length() - 1, share.bit_length() - 1
    kv_of_row = (lax.broadcasted_iota(jnp.int32, (tile, width), 0) & (heads - 1)) >> share_bits
    mine = [jnp.where(kv_of_row == g, 1.0, 0.0).astype(F32) for g in range(kv_heads)]

    def spread(k_ref, v_ref):
        for src, dst in ((k_ref, k_near), (v_ref, v_near)):
            wide[pl.ds(0, cols), :] = src[...].astype(F32)
            for g in range(kv_heads):
                dst[:, g * width : (g + 1) * width] = wide[pl.ds(g, tok, stride=kv_heads), :].astype(BF16)

    def weigh(p, depth):
        both = dot(p, v_near[pl.ds(0, depth), :], (1, 0))
        own = sum(both[:, g * width : (g + 1) * width] * mine[g] for g in range(kv_heads))
        return own, both[:, kv_heads * width :]

    def own_block():
        mask_bf = [m.astype(BF16) for m in mine]
        for i in range(rows // tile):
            for g in range(kv_heads):
                q_wide[pl.ds(i * tile, tile), g * width : (g + 1) * width] = qs[pl.ds(i * tile, tile), :] * mask_bf[g]
        v_near[:, kv_heads * width :] = jnp.ones((tok, width), BF16)
        spread(ks, vs)
        for i in range(rows // tile):
            at = pl.ds(i * tile, tile)
            depth = min(tok, -(-(i + 1) * span // width) * width)
            s = dot(q_wide[at, :], k_near[pl.ds(0, depth), :], (1, 1))
            token = (lax.broadcasted_iota(jnp.int32, (tile, depth), 0) >> head_bits) + i * span
            s = jnp.where(lax.broadcasted_iota(jnp.int32, (tile, depth), 1) <= token, s, NEVER)
            high = jnp.max(s, axis=1, keepdims=True)
            p = jnp.exp2((s - high) * c2).astype(BF16)
            top[at, :] = jnp.broadcast_to(high, (tile, width))
            own, size = weigh(p, depth)
            acc[at, :width] = own
            acc[at, width:] = size

    def held_block(slot):
        bias = jnp.where(doc_of(slot * tok) == my_doc, 0.0, NEVER).astype(F32)
        spread(k_held.at[slot], v_held.at[slot])

        for i in range(rows // tile):
            at = pl.ds(i * tile, tile)
            s = dot(q_wide[at, :], k_near[...], (1, 1)) + bias
            before = top[at, :]
            high = jnp.maximum(before, jnp.max(s, axis=1, keepdims=True))
            p = jnp.exp2((s - high[:, :1]) * c2).astype(BF16)
            shrink = jnp.exp2((before - high) * c2)
            top[at, :] = high
            own, size = weigh(p, tok)
            acc[at, :width] = acc[at, :width] * shrink + own
            acc[at, width:] = acc[at, width:] * shrink + size

    def arrive(slot):
        for incoming, outgoing in zip(passes(slot), passes(slot)):
            incoming.wait_recv()

            @pl.when(sends)
            def _():
                outgoing.start()

    for load in loads[4:]:
        load.wait()
    own_block()

    @pl.when(takes)
    def _():
        arrive(me - 1)

    loads[3].wait()
    by_head(ql, q_head)
    for c in range(heads // chunk):
        for h in range(c * chunk, (c + 1) * chunk):
            gap = jnp.where(lower, rise[:, h : h + 1] - rise_t[h : h + 1, :], NEVER)
            inner = (dot(q_head[h], k_head[h], (1, 1)) * jnp.exp(gap)).astype(BF16)
            intra[h] = dot(inner, v_head[h], (1, 0))

        @pl.when(takes & sends)
        def _():
            state_push(c).wait_recv()
            for h in range(c * chunk, (c + 1) * chunk):
                joined = s_held[h].astype(F32) * block_factor[:, h : h + 1] + local_state[h]
                s_own[h] = (keep_next * joined).astype(BF16)
            state_push(c).start()

    @pl.when(takes)
    def _():
        held_block(me - 1)

        def step(k, _):
            slot = me - k
            arrive(slot)
            held_block(slot)
            return 0

        lax.fori_loop(2, me + 1, step, 0)

    soft_out[...] = (acc[:, :width] / acc[:, width:]).astype(BF16)
    soft_store = pltpu.make_async_copy(soft_out, soft_hbm, out_sems.at[0])
    soft_store.start()

    def finish(h, total):
        size = jnp.mean(total * total, axis=1, keepdims=True)
        wide[pl.ds(h, tok, stride=heads), :] = total * lax.rsqrt(size + 1e-6)

    @pl.when(takes)
    def _():
        for c in range(heads // chunk):
            @pl.when(jnp.logical_not(sends))
            def _():
                state_push(c).wait_recv()

            for h in range(c * chunk, (c + 1) * chunk):
                finish(h, intra[h] + from_start[:, h : h + 1] * dot(q_head[h], s_held[h], (1, 0)))

    @pl.when(jnp.logical_not(takes))
    def _():
        for h in range(heads):
            finish(h, intra[h])

    lin_stores = []
    for i in range(PIECES):
        part = pl.ds(i * (rows // PIECES), rows // PIECES)
        lin_out[part, :] = wide[part, :].astype(BF16)
        lin_stores.append(pltpu.make_async_copy(lin_out.at[part], lin_hbm.at[part], out_sems.at[1 + i]))
        lin_stores[i].start()

    @pl.when(sends)
    def _():
        for copy in own_pushes():
            copy.wait_send()
        for c in range(heads // chunk):
            state_push(c).wait_send()

        def step(slot, _):
            for copy in passes(slot):
                copy.wait_send()
            return 0

        lax.fori_loop(0, me, step, 0)

    soft_store.wait()
    for store in lin_stores:
        store.wait()


def hand_over(lin, soft, lin_out, soft_out, lin_near, soft_near, in_sems, out_sems):
    size = lin.shape[0] // PIECES
    loads, stores = [], []
    for i in range(PIECES):
        part = pl.ds(i * size, size)
        for j, (src, near, dst) in enumerate([(lin, lin_near, lin_out), (soft, soft_near, soft_out)]):
            loads.append(pltpu.make_async_copy(src.at[part], near.at[part], in_sems.at[j, i]))
            stores.append(pltpu.make_async_copy(near.at[part], dst.at[part], out_sems.at[j, i]))
    for load in loads:
        load.start()
    for load, store in zip(loads, stores):
        load.wait()
        store.start()
    for store in stores:
        store.wait()


def on_device(n, q_lin, k_lin, v_lin, decay_log, q_soft, k_soft, v_soft, doc_starts):
    tok, heads, width = q_lin.shape
    kv_heads = k_soft.shape[1]
    rows, cols, slots = tok * heads, tok * kv_heads, max(n - 2, 1)
    chunk = 2
    flat = lambda x: x.reshape(-1, width)
    hbm = pl.BlockSpec(memory_space=pl.ANY)
    vmem = pltpu.VMEM
    dma = pltpu.SemaphoreType.DMA
    lin, soft = pl.pallas_call(
        functools.partial(kernel, n, tok, heads, kv_heads, q_soft.shape[1] // kv_heads, chunk),
        out_shape=[jax.ShapeDtypeStruct((rows, width), BF16)] * 2,
        in_specs=[pl.BlockSpec(memory_space=pltpu.SMEM)] + [hbm] * 7,
        out_specs=[hbm, hbm],
        scratch_shapes=[
            vmem((rows, width), BF16), vmem((rows, width), BF16), vmem((rows, width), BF16),
            vmem((heads, tok), F32), vmem((rows, width), BF16), vmem((cols, width), BF16), vmem((cols, width), BF16),
            vmem((rows, kv_heads * width), BF16), vmem((tok, kv_heads * width), BF16), vmem((tok, (kv_heads + 1) * width), BF16),
            vmem((rows, width), BF16), vmem((rows, width), BF16),
            vmem((slots, cols, width), BF16), vmem((slots, cols, width), BF16),
            vmem((heads, width, width), BF16), vmem((heads, width, width), BF16), vmem((heads, width, width), F32),
            vmem((rows, width), F32),
            vmem((heads, tok, width), BF16), vmem((heads, tok, width), BF16), vmem((heads, tok, width), BF16),
            vmem((heads, tok, width), F32),
            vmem((rows, width), F32), vmem((rows, 2 * width), F32),
            dma((7,)), dma((1 + PIECES,)), dma((2,)), dma((slots, 2)), dma((slots, 2)),
            dma((heads // chunk,)), dma((heads // chunk,)),
        ],
        compiler_params=pltpu.CompilerParams(
            collective_id=0, has_side_effects=True, vmem_limit_bytes=GRANT
        ),
        cost_estimate=pl.CostEstimate(flops=2_000_000_000, bytes_accessed=4_000_000, transcendentals=4_000_000),
    )(doc_starts, flat(q_lin), flat(k_lin), flat(v_lin), decay_log.T, flat(q_soft), flat(k_soft), flat(v_soft))
    lin, soft = pl.pallas_call(
        hand_over,
        out_shape=[jax.ShapeDtypeStruct((rows, width), BF16)] * 2,
        in_specs=[pl.BlockSpec(memory_space=pl.ANY)] * 2,
        out_specs=[pl.BlockSpec(memory_space=pl.ANY)] * 2,
        scratch_shapes=[vmem((rows, width), BF16), vmem((rows, width), BF16), dma((2, PIECES)), dma((2, PIECES))],
        compiler_params=pltpu.CompilerParams(vmem_limit_bytes=GRANT),
    )(lin, soft)
    return lin.reshape(q_lin.shape), soft.reshape(q_soft.shape)


def solution(mesh):
    long = P(("group", "ctx"), ("head", "sub"), None)
    return jax.shard_map(
        functools.partial(on_device, mesh.shape["ctx"]),
        mesh=mesh,
        in_specs=(long, long, long, P(("group", "ctx"), ("head", "sub")), long, long, long, P("group")),
        out_specs=(long, long),
        check_vma=False,
    )
```

```python
import functools
import math

import jax
import jax.numpy as jnp
from jax import lax
from jax.experimental import pallas as pl
from jax.experimental.pallas import tpu as pltpu
from jax.sharding import PartitionSpec as P

MESH = pl.DeviceIdType.MESH
F32, BF16 = jnp.float32, jnp.bfloat16
NEVER = -1e30
PIECES = 4
GRANT = 60 * 1024 * 1024


def dot(a, b, contract):
    return lax.dot_general(a, b, ((contract[:1], contract[1:]), ((), ())), preferred_element_type=F32)


def kernel(n, tok, heads, kv_heads, share, chunk, starts, ql_hbm, kl_hbm, vl_hbm, decay_hbm, qs_hbm, ks_hbm, vs_hbm,
           lin_hbm, soft_hbm,
           ql, kl, vl, decay, qs, ks, vs, q_wide, k_near, v_near, lin_out, soft_out,
           k_held, v_held, s_held, s_own, local_state, wide, q_head, k_head, v_head, intra, top, acc,
           in_sems, out_sems, own_sems, pass_sems, kv_sems, s_send, s_recv):
    me = lax.axis_index("ctx")
    sends = me < n - 2
    takes = (me > 0) & (me < n - 1)
    right, left = me + 1, me - 1
    rows, cols = tok * heads, tok * kv_heads

    barrier = pltpu.get_barrier_semaphore()

    @pl.when(sends)
    def _():
        pl.semaphore_signal(barrier, inc=1, device_id={"ctx": right}, device_id_type=MESH)

    @pl.when(takes)
    def _():
        pl.semaphore_signal(barrier, inc=1, device_id={"ctx": left}, device_id_type=MESH)

    loads = [
        pltpu.make_async_copy(src, dst, in_sems.at[i])
        for i, (src, dst) in enumerate(
            [(decay_hbm, decay), (kl_hbm, kl), (vl_hbm, vl), (ql_hbm, ql), (qs_hbm, qs), (ks_hbm, ks), (vs_hbm, vs)]
        )
    ]
    for load in loads:
        load.start()

    @pl.when(sends & takes)
    def _():
        pl.semaphore_wait(barrier, 2)

    @pl.when(sends != takes)
    def _():
        pl.semaphore_wait(barrier, 1)

    def push(src, dst, send_sem, recv_sem):
        return pltpu.make_async_remote_copy(
            src_ref=src, dst_ref=dst, send_sem=send_sem, recv_sem=recv_sem,
            device_id={"ctx": right}, device_id_type=MESH,
        )

    def own_pushes():
        return (
            push(ks_hbm, k_held.at[me], own_sems.at[0], kv_sems.at[me, 0]),
            push(vs_hbm, v_held.at[me], own_sems.at[1], kv_sems.at[me, 1]),
        )

    def passes(slot):
        return (
            push(k_held.at[slot], k_held.at[slot], pass_sems.at[slot, 0], kv_sems.at[slot, 0]),
            push(v_held.at[slot], v_held.at[slot], pass_sems.at[slot, 1], kv_sems.at[slot, 1]),
        )

    def state_push(c):
        part = pl.ds(c * chunk, chunk)
        return push(s_own.at[part], s_held.at[part], s_send.at[c], s_recv.at[c])

    @pl.when(sends)
    def _():
        own_pushes()[0].start()

    @pl.when(takes & sends)
    def _():
        own_pushes()[1].start()

    def doc_of(position):
        return sum((starts[i] <= position).astype(jnp.int32) for i in range(starts.shape[0]))

    my_doc = doc_of(me * tok)
    keep_next = jnp.where(my_doc == doc_of((me + 1) * tok), 1.0, 0.0).astype(F32)

    loads[0].wait()
    d = decay[...]
    d1 = d.astype(BF16)
    rest = d - d1.astype(F32)
    d2 = rest.astype(BF16)
    d3 = (rest - d2.astype(F32)).astype(BF16)
    i_row = lax.broadcasted_iota(jnp.int32, (tok, tok), 0)
    i_col = lax.broadcasted_iota(jnp.int32, (tok, tok), 1)
    lower = i_row >= i_col
    tri = jnp.where(lower, 1.0, 0.0).astype(BF16)
    rise = dot(tri, d1, (1, 1)) + dot(tri, d2, (1, 1)) + dot(tri, d3, (1, 1))
    rise_t = dot(d1, tri, (1, 1)) + dot(d2, tri, (1, 1)) + dot(d3, tri, (1, 1))
    last = rise[tok - 1 :, :]
    to_end = jnp.exp(last - rise)
    from_start = jnp.exp(rise)
    block_factor = jnp.exp(last)

    def by_head(src, dst):
        wide[...] = src[...].astype(F32)
        for h in range(heads):
            dst[h] = wide[pl.ds(h, tok, stride=heads), :].astype(BF16)

    loads[1].wait()
    by_head(kl, k_head)

    @pl.when(me == 0)
    def _():
        own_pushes()[1].start()

    loads[2].wait()
    by_head(vl, v_head)

    @pl.when(sends)
    def _():
        for h in range(heads):
            tail = (k_head[h].astype(F32) * to_end[:, h : h + 1]).astype(BF16)
            local_state[h] = dot(tail, v_head[h], (0, 0))

    @pl.when(me == 0)
    def _():
        for c in range(heads // chunk):
            for h in range(c * chunk, (c + 1) * chunk):
                s_own[h] = (keep_next * local_state[h]).astype(BF16)
            state_push(c).start()

    width = qs.shape[1]
    c2 = math.log2(math.e) / math.sqrt(width)
    tile = min(256, rows)
    span = tile // heads
    head_bits, share_bits = heads.bit_length() - 1, share.bit_length() - 1
    kv_of_row = (lax.broadcasted_iota(jnp.int32, (tile, width), 0) & (heads - 1)) >> share_bits
    mine = [jnp.where(kv_of_row == g, 1.0, 0.0).astype(F32) for g in range(kv_heads)]

    def spread(k_ref, v_ref):
        for src, dst in ((k_ref, k_near), (v_ref, v_near)):
            wide[pl.ds(0, cols), :] = src[...].astype(F32)
            for g in range(kv_heads):
                dst[:, g * width : (g + 1) * width] = wide[pl.ds(g, tok, stride=kv_heads), :].astype(BF16)

    def weigh(p, depth):
        both = dot(p, v_near[pl.ds(0, depth), :], (1, 0))
        own = sum(both[:, g * width : (g + 1) * width] * mine[g] for g in range(kv_heads))
        return own, both[:, kv_heads * width :]

    def own_block():
        mask_bf = [m.astype(BF16) for m in mine]
        for i in range(rows // tile):
            for g in range(kv_heads):
                q_wide[pl.ds(i * tile, tile), g * width : (g + 1) * width] = qs[pl.ds(i * tile, tile), :] * mask_bf[g]
        v_near[:, kv_heads * width :] = jnp.ones((tok, width), BF16)
        spread(ks, vs)
        for i in range(rows // tile):
            at = pl.ds(i * tile, tile)
            depth = min(tok, -(-(i + 1) * span // width) * width)
            s = dot(q_wide[at, :], k_near[pl.ds(0, depth), :], (1, 1))
            token = (lax.broadcasted_iota(jnp.int32, (tile, depth), 0) >> head_bits) + i * span
            s = jnp.where(lax.broadcasted_iota(jnp.int32, (tile, depth), 1) <= token, s, NEVER)
            high = jnp.max(s, axis=1, keepdims=True)
            p = jnp.exp2((s - high) * c2).astype(BF16)
            top[at, :] = jnp.broadcast_to(high, (tile, width))
            own, size = weigh(p, depth)
            acc[at, :width] = own
            acc[at, width:] = size

    def held_block(slot):
        bias = jnp.where(doc_of(slot * tok) == my_doc, 0.0, NEVER).astype(F32)
        spread(k_held.at[slot], v_held.at[slot])

        for i in range(rows // tile):
            at = pl.ds(i * tile, tile)
            s = dot(q_wide[at, :], k_near[...], (1, 1)) + bias
            before = top[at, :]
            high = jnp.maximum(before, jnp.max(s, axis=1, keepdims=True))
            p = jnp.exp2((s - high[:, :1]) * c2).astype(BF16)
            shrink = jnp.exp2((before - high) * c2)
            top[at, :] = high
            own, size = weigh(p, tok)
            acc[at, :width] = acc[at, :width] * shrink + own
            acc[at, width:] = acc[at, width:] * shrink + size

    def arrive(slot):
        for incoming, outgoing in zip(passes(slot), passes(slot)):
            incoming.wait_recv()

            @pl.when(sends)
            def _():
                outgoing.start()

    for load in loads[4:]:
        load.wait()
    own_block()

    @pl.when(takes)
    def _():
        arrive(me - 1)

    loads[3].wait()
    by_head(ql, q_head)
    for c in range(heads // chunk):
        for h in range(c * chunk, (c + 1) * chunk):
            gap = jnp.where(lower, rise[:, h : h + 1] - rise_t[h : h + 1, :], NEVER)
            inner = (dot(q_head[h], k_head[h], (1, 1)) * jnp.exp(gap)).astype(BF16)
            intra[h] = dot(inner, v_head[h], (1, 0))

        @pl.when(takes & sends)
        def _():
            state_push(c).wait_recv()
            for h in range(c * chunk, (c + 1) * chunk):
                joined = s_held[h].astype(F32) * block_factor[:, h : h + 1] + local_state[h]
                s_own[h] = (keep_next * joined).astype(BF16)
            state_push(c).start()

    @pl.when(takes)
    def _():
        held_block(me - 1)

        def step(k, _):
            slot = me - k
            arrive(slot)
            held_block(slot)
            return 0

        lax.fori_loop(2, me + 1, step, 0)

    soft_out[...] = (acc[:, :width] / acc[:, width:]).astype(BF16)
    soft_store = pltpu.make_async_copy(soft_out, soft_hbm, out_sems.at[0])
    soft_store.start()

    def finish(h, total):
        size = jnp.mean(total * total, axis=1, keepdims=True)
        wide[pl.ds(h, tok, stride=heads), :] = total * lax.rsqrt(size + 1e-6)

    @pl.when(takes)
    def _():
        for c in range(heads // chunk):
            @pl.when(jnp.logical_not(sends))
            def _():
                state_push(c).wait_recv()

            for h in range(c * chunk, (c + 1) * chunk):
                finish(h, intra[h] + from_start[:, h : h + 1] * dot(q_head[h], s_held[h], (1, 0)))

    @pl.when(jnp.logical_not(takes))
    def _():
        for h in range(heads):
            finish(h, intra[h])

    lin_stores = []
    for i in range(PIECES):
        part = pl.ds(i * (rows // PIECES), rows // PIECES)
        lin_out[part, :] = wide[part, :].astype(BF16)
        lin_stores.append(pltpu.make_async_copy(lin_out.at[part], lin_hbm.at[part], out_sems.at[1 + i]))
        lin_stores[i].start()

    @pl.when(sends)
    def _():
        for copy in own_pushes():
            copy.wait_send()
        for c in range(heads // chunk):
            state_push(c).wait_send()

        def step(slot, _):
            for copy in passes(slot):
                copy.wait_send()
            return 0

        lax.fori_loop(0, me, step, 0)

    soft_store.wait()
    for store in lin_stores:
        store.wait()


def hand_over(lin, soft, lin_out, soft_out, lin_near, soft_near, in_sems, out_sems):
    size = lin.shape[0] // PIECES
    loads, stores = [], []
    for i in range(PIECES):
        part = pl.ds(i * size, size)
        for j, (src, near, dst) in enumerate([(lin, lin_near, lin_out), (soft, soft_near, soft_out)]):
            loads.append(pltpu.make_async_copy(src.at[part], near.at[part], in_sems.at[j, i]))
            stores.append(pltpu.make_async_copy(near.at[part], dst.at[part], out_sems.at[j, i]))
    for load in loads:
        load.start()
    for load, store in zip(loads, stores):
        load.wait()
        store.start()
    for store in stores:
        store.wait()


def on_device(n, q_lin, k_lin, v_lin, decay_log, q_soft, k_soft, v_soft, doc_starts):
    tok, heads, width = q_lin.shape
    kv_heads = k_soft.shape[1]
    rows, cols, slots = tok * heads, tok * kv_heads, max(n - 2, 1)
    chunk = 2
    flat = lambda x: x.reshape(-1, width)
    hbm = pl.BlockSpec(memory_space=pl.ANY)
    vmem = pltpu.VMEM
    dma = pltpu.SemaphoreType.DMA
    lin, soft = pl.pallas_call(
        functools.partial(kernel, n, tok, heads, kv_heads, q_soft.shape[1] // kv_heads, chunk),
        out_shape=[jax.ShapeDtypeStruct((rows, width), BF16)] * 2,
        in_specs=[pl.BlockSpec(memory_space=pltpu.SMEM)] + [hbm] * 7,
        out_specs=[hbm, hbm],
        scratch_shapes=[
            vmem((rows, width), BF16), vmem((rows, width), BF16), vmem((rows, width), BF16),
            vmem((heads, tok), F32), vmem((rows, width), BF16), vmem((cols, width), BF16), vmem((cols, width), BF16),
            vmem((rows, kv_heads * width), BF16), vmem((tok, kv_heads * width), BF16), vmem((tok, (kv_heads + 1) * width), BF16),
            vmem((rows, width), BF16), vmem((rows, width), BF16),
            vmem((slots, cols, width), BF16), vmem((slots, cols, width), BF16),
            vmem((heads, width, width), BF16), vmem((heads, width, width), BF16), vmem((heads, width, width), F32),
            vmem((rows, width), F32),
            vmem((heads, tok, width), BF16), vmem((heads, tok, width), BF16), vmem((heads, tok, width), BF16),
            vmem((heads, tok, width), F32),
            vmem((rows, width), F32), vmem((rows, 2 * width), F32),
            dma((7,)), dma((1 + PIECES,)), dma((2,)), dma((slots, 2)), dma((slots, 2)),
            dma((heads // chunk,)), dma((heads // chunk,)),
        ],
        compiler_params=pltpu.CompilerParams(
            collective_id=0, has_side_effects=True, vmem_limit_bytes=GRANT
        ),
        cost_estimate=pl.CostEstimate(flops=2_000_000_000, bytes_accessed=4_000_000, transcendentals=4_000_000),
    )(doc_starts, flat(q_lin), flat(k_lin), flat(v_lin), decay_log.T, flat(q_soft), flat(k_soft), flat(v_soft))
    lin, soft = pl.pallas_call(
        hand_over,
        out_shape=[jax.ShapeDtypeStruct((rows, width), BF16)] * 2,
        in_specs=[pl.BlockSpec(memory_space=pl.ANY)] * 2,
        out_specs=[pl.BlockSpec(memory_space=pl.ANY)] * 2,
        scratch_shapes=[vmem((rows, width), BF16), vmem((rows, width), BF16), dma((2, PIECES)), dma((2, PIECES))],
        compiler_params=pltpu.CompilerParams(vmem_limit_bytes=GRANT),
    )(lin, soft)
    return lin.reshape(q_lin.shape), soft.reshape(q_soft.shape)


def solution(mesh):
    long = P(("group", "ctx"), ("head", "sub"), None)
    return jax.shard_map(
        functools.partial(on_device, mesh.shape["ctx"]),
        mesh=mesh,
        in_specs=(long, long, long, P(("group", "ctx"), ("head", "sub")), long, long, long, P("group")),
        out_specs=(long, long),
        check_vma=False,
    )
```
